128 devices in a mesh: orb: 16 (over y_lo, z, core), dom: 8 (over y_hi, x).
Axes of the slice: x: 4, y: 4 (y_hi: 2, y_lo: 2; y = y_hi * 2 + y_lo), z: 4, core: 2. Of those that a mesh axis runs over, the one named last changes fastest.
Arguments:
- orbitals: float32 [128, 64, 64, 128], P('orb', 'dom'), may hold values from -6 to 6
- veff: float32 [64, 64, 128], P('dom'), may hold values from -1 to 0
- trials: float32 [16, 64, 64, 128], P('orb', 'dom'), may hold values from -32 to 32
- owners: int32 [2], replicated, may hold values from 0 to 15
- levels: float32 [8], replicated, may hold values from 0.05 to 1
- shift_index: int32 [128], P('orb'), may hold values from 0 to 7
Outputs:
- responses: float32 [16, 64, 64, 128], P('orb', 'dom')
The draws below stay inside these ranges and needn't reach their ends.
Inputs may be any that keep to these rules, and one draw needn't show every extreme that they name: `owners`: an orbital group index. `shift_index`: an index into levels.
All inputs are finite; a program needn't handle non-finite values.
Results may differ from the reference program's by a relative error of at most 0.0001.
Values sent between devices are 32-bit elements; how exact they have to be, the bound alone decides.
A program may use at most 128 MiB of HBM per device.

```python
import math
import jax
import jax.numpy as jnp
from jax import lax

NY = 64
NZ = 128
APPS = 2
SWEEPS = 4
LEVELS = 8
NX = 64
NORB = 128
SLOTS = 16


def draw_trials(key, part):
    first = jax.random.fold_in(jax.random.fold_in(key, 17), 0)
    position = jnp.arange(NX, dtype=jnp.float32) / (NX - 1)
    rising = jnp.exp(0.5 * math.log(3.0) * position)[None, :, None, None]
    return jnp.clip(jax.random.normal(first, (SLOTS, NX, NY, NZ), jnp.float32) * rising, -32.0, 32.0)


def place_ends(result, own_key, low, largest):
    place = [jax.random.randint(jax.random.fold_in(own_key, axis), (), 0, length) for axis, length in enumerate(result.shape)]
    widest = result.shape.index(max(result.shape))
    neighbour = place[:widest] + [(place[widest] + 1) % result.shape[widest]] + place[widest + 1:]
    return result.at[tuple(place)].set(low).at[tuple(neighbour)].set(largest)


def block_levels(stream_key, shape, cuts, least, top_value):
    factor_of, own = 1.0, jax.random.fold_in(stream_key, 6)
    for dim, shards_of in cuts:
        draws = jnp.exp(jax.random.uniform(jax.random.fold_in(own, dim), (shards_of,), jnp.float32, least / len(cuts), top_value / len(cuts)))
        factor_of = factor_of * jnp.repeat(draws, shape[dim] // shards_of).reshape([-1 if axis == dim else 1 for axis in range(len(shape))])
    return factor_of


def scatter_about(key, dims, spread, reach, cuts=(), kind=jnp.bfloat16):
    array = spread * jax.random.normal(key, dims, jnp.float32)
    if cuts:
        array = array * block_levels(key, dims, cuts, -0.22, 0.18)
    return jnp.clip(array, -reach, reach).astype(kind)


def setup_inputs(seed: int = 0) -> dict:
    key_of = jax.random.split(jax.random.key(seed), 7)
    return {
        "orbitals": scatter_about(key_of[0], (NORB, NX, NY, NZ), 1.0, 6.0, ((0, 16), (1, 8)), jnp.float32),
        "veff": jnp.clip(-1.0 + 1.0 * jax.random.uniform(key_of[1], (NX, NY, NZ), jnp.float32) ** block_levels(key_of[1], (NX, NY, NZ), ((0, 8),), -0.2, 0.2), -1.0, 0.0),
        "trials": draw_trials(jax.random.fold_in(key_of[6], 71), 0),
        "owners": jax.random.randint(key_of[3], (APPS,), 0, SLOTS).astype(jnp.int32),
        "levels": jnp.clip(jnp.exp(jax.random.uniform(key_of[4], (LEVELS,), jnp.float32, math.log(0.05), math.log(1.0))), 0.05, 1.0),
        "shift_index": place_ends(jax.random.randint(key_of[5], (NORB,), 0, LEVELS), jax.random.fold_in(key_of[5], 1), 0, LEVELS - 1).astype(jnp.int32),
    }


stencil_taps = (-49.0 / 18.0, 1.5, -0.15, 1.0 / 90.0)
center_shift = 4.05
center_depth = 5.05
inverse_half = 1.0 / 5.05
norm_epsilon = 1e-06

def apply_map(extended, potential_in):
    inner_count = extended.shape[1] - 6
    width_y = extended.shape[2]
    width_z = extended.shape[3]
    padded = jnp.pad(extended, ((0, 0), (0, 0), (3, 3), (3, 3)))
    middle = padded[:, 3:3 + inner_count, 3:3 + width_y, 3:3 + width_z]
    laplace = 3.0 * stencil_taps[0] * middle
    for offset in (1, 2, 3):
        weight = stencil_taps[offset]
        laplace = laplace + weight * (padded[:, 3 + offset:3 + offset + inner_count, 3:3 + width_y, 3:3 + width_z] + padded[:, 3 - offset:3 - offset + inner_count, 3:3 + width_y, 3:3 + width_z])
        laplace = laplace + weight * (padded[:, 3:3 + inner_count, 3 + offset:3 + offset + width_y, 3:3 + width_z] + padded[:, 3:3 + inner_count, 3 - offset:3 - offset + width_y, 3:3 + width_z])
        laplace = laplace + weight * (padded[:, 3:3 + inner_count, 3:3 + width_y, 3 + offset:3 + offset + width_z] + padded[:, 3:3 + inner_count, 3:3 + width_y, 3 - offset:3 - offset + width_z])
    energy = -0.5 * laplace + potential_in[None] * middle
    return (energy - center_shift * middle) * inverse_half

def coefficients(level_gap):
    ratio_q = (center_depth + level_gap) * inverse_half
    root_term = jnp.sqrt(ratio_q * ratio_q - 1.0)
    decay = ratio_q - root_term
    first = -inverse_half / root_term
    series = [first]
    current = first * (-2.0 * decay)
    series.append(current)
    for offset in range(2, SWEEPS + 1):
        current = current * -decay
        series.append(current)
    return series

def global_map(field, veff):
    extended = jnp.pad(field[None], ((0, 0), (3, 3), (0, 0), (0, 0)))
    return apply_map(extended, veff)[0]

def filtered(initial, veff, series):
    summed = series[0] * initial
    previous = initial
    current = global_map(initial, veff)
    summed = summed + series[1] * current
    for offset in range(2, SWEEPS + 1):
        following = 2.0 * global_map(current, veff) - previous
        summed = summed + series[offset] * following
        previous = current
        current = following
    return summed

def reference(orbitals, veff, trials, owners, levels, shift_index):
    grid_cells = NX * NY * NZ
    level_gaps = levels[shift_index]
    responses = jnp.zeros((SLOTS, NX, NY, NZ), jnp.float32)
    slot_ids = jnp.arange(SLOTS, dtype=jnp.int32)
    for app_index in range(APPS):
        chosen_trial = lax.dynamic_index_in_dim(trials, owners[app_index], 0, keepdims=False)
        potential = chosen_trial * lax.rsqrt(jnp.sum(chosen_trial * chosen_trial) / grid_cells + norm_epsilon)

        def add_orbital(running, inputs):
            orbital, level_gap = inputs
            series = coefficients(level_gap)
            delta = filtered(potential * orbital, veff, series)
            return (running + orbital * delta, None)
        running, unused = lax.scan(add_orbital, jnp.zeros((NX, NY, NZ), jnp.float32), (orbitals, level_gaps))
        response = running * (4.0 / NORB)
        chosen = (slot_ids == owners[app_index])[:, None, None, None]
        responses = responses + jnp.where(chosen, response[None], 0.0)
    return responses
```

```python
import functools

import jax
import jax.numpy as jnp
import numpy as np
from jax import lax
from jax.experimental import pallas as pl
from jax.experimental.pallas import tpu as pltpu
from jax.sharding import PartitionSpec as P

APPS = 2
SWEEPS = 4
MESH = pl.DeviceIdType.MESH

taps = (135.0, -13.5, 1.0)
inverse_half = 1.0 / 5.05
center_depth = 5.05
norm_epsilon = 1e-06
beta = -0.5 * inverse_half / 90.0
center_rest = 49.0 / 12.0 - 4.05

XP, YP, ZP = 2, 1, 0
GROUPS = ((0, 24), (24, 24), (48, 16))


def place():
    orb, dom = lax.axis_index("orb"), lax.axis_index("dom")
    return dom % 4, dom // 4, orb // 8, (orb // 2) % 4, orb % 2


def device(x, y, z, c):
    return ((y % 2) * 8 + z * 2 + c, (y // 2) * 4 + x)


class Copies:
    def __init__(self, send, recv):
        self.send, self.recv, self.count = send, recv, 0

    def remote(self, src, dst, target):
        at = self.count
        self.count += 1
        copy = pltpu.make_async_remote_copy(
            src_ref=src,
            dst_ref=dst,
            send_sem=self.send.at[at],
            recv_sem=self.recv.at[at],
            device_id=target,
            device_id_type=MESH,
        )
        copy.start()
        return copy

    def local(self, src, dst):
        at = self.count
        self.count += 1
        copy = pltpu.make_async_copy(src, dst, self.send.at[at])
        copy.start()
        return copy


SEMS = 160


def kernel(
    orbitals, veff, trials, table, band, out,
    phi, vfull, geff, masked, scattered, coef, fields, work_a, work_b, resp,
    r0a, r1a, r2a, r0b, r1b, r2b, r0c, r1c, r2c, s0a, s1a, s2a, s0b, s1b, s2b, final, slabs,
    send, recv,
):
    x, yh, yl, z, c = place()
    y = 2 * yh + yl
    orb, dom = lax.axis_index("orb"), lax.axis_index("dom")
    own = yl * 4 + z
    copies = Copies(send, recv)

    def along(dim, r):
        if dim == XP:
            return device((x + r) % 4, y, z, c)
        if dim == YP:
            return device(x, (y + r) % 4, z, c)
        return device(x, y, (z + r) % 4, c)

    sibling = device(x, y, z, 1 - c)

    barrier = pltpu.get_barrier_semaphore()
    peers = [((orb + r) % 16, dom) for r in range(1, 16)]
    peers += [(orb, (dom + r) % 8) for r in range(1, 8)]
    peers += [along(YP, 1), along(YP, 3)]
    for peer in peers:
        pl.semaphore_signal(barrier, inc=1, device_id=peer, device_id_type=MESH)
    pl.semaphore_wait(barrier, len(peers))

    for app in range(APPS):
        for i in range(8):
            masked[app, i] = trials[0, i] * table[8, app : app + 1, :]
    spread = []
    for r in range(1, 16):
        to = (orb + r) % 16
        spread.append(copies.remote(masked.at[to % 2, to // 2], scattered.at[orb], (to, dom)))
    half = pl.ds(c * 32, 32)
    piece = veff.at[own, half]
    veff_x = [copies.remote(piece, geff.at[yh, x, yl, z, half], along(XP, r)) for r in (1, 3, 2)]
    veff_own = copies.local(piece, geff.at[yh, x, yl, z, half])
    moved = []
    for r in (4, 6, 5, 7, 2, 1, 3):
        to = (dom + r) % 8
        moved.append((r, copies.remote(orbitals.at[to], phi.at[c, dom], (orb, to))))
    phi_own = copies.local(orbitals.at[dom], phi.at[c, dom])
    phi_pair = [copies.remote(orbitals.at[dom], phi.at[c, dom], sibling)]
    coef_own = copies.local(table.at[dom], coef.at[c])
    coef_pair = copies.remote(table.at[dom], coef.at[c], sibling)

    zero_rows = jnp.zeros((8, 128), jnp.float32)
    zero_plane = jnp.zeros((80, 128), jnp.float32)
    for buffer in (fields, work_a, work_b):
        for k in range(2):
            for p in (0, 1, 2, 67, 68, 69):
                buffer[k, p] = zero_plane

            def border(p, carry, buffer=buffer, k=k):
                buffer[k, p, 0:8] = zero_rows
                buffer[k, p, 72:80] = zero_rows
                return carry

            lax.fori_loop(3, 67, border, 0)

    scattered[orb] = masked[c, own]
    for copy in spread:
        copy.wait()
    total = scattered[0]
    for g in range(1, 16):
        total = total + scattered[g]
    vfull[yh, x, yl, z] = total
    v_x = [copies.remote(vfull.at[yh, x, yl, z], vfull.at[yh, x, yl, z], along(XP, r)) for r in (1, 3, 2)]

    veff_own.wait()
    for copy in veff_x:
        copy.wait()
    row = geff.at[yh, :, yl, z, half]
    veff_y = [copies.remote(row, row, along(YP, r)) for r in (1, 3, 2)]
    for copy in v_x:
        copy.wait()
    row = vfull.at[yh, :, yl, z]
    v_y = [copies.remote(row, row, along(YP, r)) for r in (1, 3, 2)]
    for copy in veff_y:
        copy.wait()
    pairs = []

    def ring(at):
        block = at(z, None)
        return [copies.remote(block, block, along(ZP, r)) for r in (1, 3)]

    def relay(at, sends):
        for copy in sends:
            copy.wait()
        first, second = at((z + 3) % 4, 0), at((z + 1) % 4, 1)
        return [copies.remote(first, first, along(ZP, 1)), copies.remote(second, second, along(ZP, 3))]

    def at_g(zz, part):
        if part is None:
            return geff.at[:, :, :, zz, half]
        return geff.at[part, :, :, zz, half]

    def at_v(zz, part):
        if part is None:
            return vfull.at[:, :, :, zz]
        return vfull.at[part, :, :, zz]

    g_z = ring(at_g)
    for copy in v_y:
        copy.wait()
    v_z = ring(at_v)
    g_r = relay(at_g, g_z)
    v_r = relay(at_v, v_z)

    phi_own.wait()
    for r, copy in moved:
        copy.wait()
        source = phi.at[c, (dom - r + 8) % 8]
        phi_pair.append(copies.remote(source, source, sibling))
    for copy in g_r:
        copy.wait()
    everything = geff.at[:, :, :, :, half]
    g_pair = copies.remote(everything, everything, sibling)
    for copy in v_r:
        copy.wait()
    for copy in phi_pair:
        copy.wait()
    coef_own.wait()
    coef_pair.wait()
    g_pair.wait()

    def start(p, norm):
        h, a, b, d = p // 32, (p // 8) % 4, (p // 4) % 2, p % 4
        v = vfull[h, a, b, d]
        for k in range(2):
            fields[k, p + 3, 8:72] = v * phi[k, p // 8, p % 8]
        geff[h, a, b, d] = (geff[h, a, b, d] + center_rest) * -180.0
        sq = v * v
        return norm + jnp.sum(sq.reshape(8, 8, 128), axis=0)

    norm = lax.fori_loop(0, 64, start, jnp.zeros((8, 128), jnp.float32))
    scale = lax.rsqrt(jnp.sum(norm, keepdims=True) * (1.0 / 524288) + norm_epsilon)

    def image(src, p, step):
        h, a, b, d = p // 32, (p // 8) % 4, (p // 4) % 2, p % 4
        both = jnp.concatenate([src[0, p + 3, 8:72], src[1, p + 3, 8:72]], axis=0)
        high = both.astype(jnp.bfloat16)
        low = (both - high.astype(jnp.float32)).astype(jnp.bfloat16)
        along_z = jnp.dot(
            jnp.concatenate([high, low], axis=1), band[...], preferred_element_type=jnp.float32
        )
        g = geff[h, a, b, d]
        results = []
        for k in range(2):
            acc = along_z[k * 64 : k * 64 + 64] + g * src[k, p + 3, 8:72]
            acc = acc + coef[k, step : step + 1, :] * fields[k, p + 3, 8:72]
            for j in (1, 2, 3):
                near = (src[k, p + 3 + j, 8:72] + src[k, p + 3 - j, 8:72]) + (
                    src[k, p + 3, 8 + j : 72 + j] + src[k, p + 3, 8 - j : 72 - j]
                )
                acc = acc + (near if j == 3 else near * taps[j - 1])
            results.append(acc)
        return results

    for step, (src, dst) in enumerate(((fields, work_a), (work_a, work_b), (work_b, work_a))):

        def sweep(p, carry, step=step, src=src, dst=dst):
            for k, value in enumerate(image(src, p, step)):
                dst[k, p + 3, 8:72] = value
            return carry

        lax.fori_loop(0, 64, sweep, 0)

    gain = [scale * coef[k, 4:5, :] for k in range(2)]

    def last(p, carry):
        h, a, b, d = p // 32, (p // 8) % 4, (p // 4) % 2, p % 4
        one, two = image(work_a, p, 3)
        resp[h, a, b, d] = one * (gain[0] * phi[0, p // 8, p % 8]) + two * (gain[1] * phi[1, p // 8, p % 8])
        return carry

    lax.fori_loop(0, 64, last, 0)

    def part(dim, r, ref, kept):
        if dim == XP:
            to = (x + r) % 4
            where = {"x": to}
        elif dim == YP:
            to = (y + r) % 4
            where = {"yh": to // 2, "yl": to % 2}
        else:
            where = {"z": (z + r) % 4}
        return ref.at[tuple(where.get(name, slice(None)) for name in kept)]

    names = {XP: ("x",), YP: ("yh", "yl"), ZP: ("z",)}
    orders = ((ZP, YP, XP), (YP, XP, ZP), (XP, ZP, YP))
    stages = ((r0a, r1a, r2a), (r0b, r1b, r2b), (r0c, r1c, r2c))
    sums = ((s0a, s1a, s2a), (s0b, s1b, s2b))
    kept = [("yh", "x", "yl", "z") for _ in GROUPS]
    current = [resp.at[:, :, :, :, first : first + count] for first, count in GROUPS]
    for stage in range(3):
        started = []
        for q in range(3):
            dim = orders[q][stage]
            started.append(
                [
                    copies.remote(part(dim, r, current[q], kept[q]), stages[stage][q].at[r - 1], along(dim, r))
                    for r in (1, 3, 2)
                ]
            )
        for q in range(3):
            dim = orders[q][stage]
            for copy in started[q]:
                copy.wait()
            received = stages[stage][q]
            mine = part(dim, 0, current[q], kept[q])
            kept[q] = tuple(name for name in kept[q] if name not in names[dim])
            first, count = GROUPS[q]
            if stage == 2:
                final[first : first + count] = (mine[...] + received[0]) + (received[1] + received[2])
            else:
                sums[stage][q][...] = (mine[...] + received[0]) + (received[1] + received[2])
                current[q] = sums[stage][q]

    slabs[c, own] = final[...]
    shared = []
    for r in range(1, 16):
        to = (orb + r) % 16
        shared.append(copies.remote(final, slabs.at[c, own], (to, dom)))
    for copy in shared:
        copy.wait()
    for i in range(8):
        out[0, i] = slabs[0, i] * table[8, 0:1, :] + slabs[1, i] * table[8, 1:2, :]


def coefficients(level_gap, orbital_count):
    ratio_q = (center_depth + level_gap) * inverse_half
    root_term = jnp.sqrt(ratio_q * ratio_q - 1.0)
    decay = ratio_q - root_term
    c0 = -inverse_half / root_term
    c1 = c0 * (-2.0 * decay)
    c2 = c1 * -decay
    c3 = c2 * -decay
    c4 = c3 * -decay
    d0, d1, d2, d3, d4 = c0 - c2 + c4, c1 - 3.0 * c3, 2.0 * c2 - 8.0 * c4, 4.0 * c3, 8.0 * c4
    inverse = 1.0 / d4
    zero = jnp.zeros_like(d0)
    rows = [
        d3 * inverse * (1.0 / beta),
        d2 * inverse * (1.0 / beta**2),
        d1 * inverse * (1.0 / beta**3),
        d0 * inverse * (1.0 / beta**4),
        d4 * (beta**4 * 4.0 / orbital_count),
        zero,
        zero,
        zero,
    ]
    return jnp.stack(rows, axis=1)


def band_matrix():
    d = np.zeros((128, 128), np.float32)
    for j, tap in enumerate(taps, 1):
        d += tap * (np.eye(128, k=j) + np.eye(128, k=-j))
    return np.concatenate([d, d], axis=0)


def per_device(orbitals, veff, trials, owners, levels, shift_index):
    orbital_count = orbitals.shape[0] * lax.axis_size("orb")
    chosen = shift_index[:, None] == jnp.arange(levels.shape[0], dtype=jnp.int32)[None, :]
    level_gaps = jnp.sum(jnp.where(chosen, levels[None, :], 0.0), axis=1)
    masks = (owners == lax.axis_index("orb")).astype(jnp.float32)
    masks = jnp.concatenate([masks, jnp.zeros((6,), jnp.float32)])
    table = jnp.concatenate([coefficients(level_gaps, orbital_count), masks[None]], axis=0)
    table = jnp.broadcast_to(table[:, :, None], (9, 8, 128))
    band = jnp.asarray(band_matrix(), jnp.bfloat16)
    f32 = jnp.float32
    vm = lambda *shape: pltpu.VMEM(shape, f32)
    full = (2, 4, 2, 4, 64, 128)
    return pl.pallas_call(
        kernel,
        out_shape=jax.ShapeDtypeStruct((1, 8, 64, 128), f32),
        in_specs=[
            pl.BlockSpec(memory_space=pl.ANY),
            pl.BlockSpec(memory_space=pl.ANY),
            pl.BlockSpec(memory_space=pltpu.VMEM),
            pl.BlockSpec(memory_space=pltpu.VMEM),
            pl.BlockSpec(memory_space=pltpu.VMEM),
        ],
        out_specs=pl.BlockSpec(memory_space=pltpu.VMEM),
        scratch_shapes=[
            vm(2, 8, 8, 64, 128),
            vm(*full),
            vm(*full),
            vm(2, 8, 64, 128),
            vm(16, 64, 128),
            vm(2, 8, 128),
            vm(2, 70, 80, 128),
            vm(2, 70, 80, 128),
            vm(2, 70, 80, 128),
            vm(*full),
            vm(3, 2, 4, 2, 24, 128),
            vm(3, 4, 4, 24, 128),
            vm(3, 2, 2, 4, 16, 128),
            vm(3, 4, 24, 128),
            vm(3, 4, 24, 128),
            vm(3, 2, 2, 16, 128),
            vm(3, 24, 128),
            vm(3, 24, 128),
            vm(3, 16, 128),
            vm(2, 4, 2, 24, 128),
            vm(4, 4, 24, 128),
            vm(2, 2, 4, 16, 128),
            vm(4, 24, 128),
            vm(4, 24, 128),
            vm(2, 2, 16, 128),
            vm(64, 128),
            vm(2, 8, 64, 128),
            pltpu.SemaphoreType.DMA((SEMS,)),
            pltpu.SemaphoreType.DMA((SEMS,)),
        ],
        compiler_params=pltpu.CompilerParams(
            collective_id=1, has_side_effects=True, vmem_limit_bytes=56 << 20
        ),
        name="response",
    )(orbitals, veff, trials, table, band)


def solution(mesh):
    placed = (
        P("orb", "dom", None, None),
        P("dom", None, None),
        P("orb", "dom", None, None),
        P(),
        P(),
        P("orb"),
    )
    return jax.shard_map(
        per_device,
        mesh=mesh,
        in_specs=placed,
        out_specs=P("orb", "dom", None, None),
        check_vma=False,
    )
```

```python
import functools

import jax
import jax.numpy as jnp
from jax import lax
from jax.experimental import pallas as pl
from jax.experimental.pallas import tpu as pltpu
from jax.sharding import PartitionSpec as P

APPS = 2
SWEEPS = 4
MESH = pl.DeviceIdType.MESH

taps = (135.0, -13.5, 1.0)
inverse_half = 1.0 / 5.05
center_depth = 5.05
norm_epsilon = 1e-06
beta = -0.5 * inverse_half / 90.0
center_rest = 49.0 / 12.0 - 4.05

XP, YP, ZP = 2, 1, 0
GROUPS = ((0, 24), (24, 24), (48, 16))


def place():
    orb, dom = lax.axis_index("orb"), lax.axis_index("dom")
    return dom % 4, dom // 4, orb // 8, (orb // 2) % 4, orb % 2


def device(x, y, z, c):
    return ((y % 2) * 8 + z * 2 + c, (y // 2) * 4 + x)


class Copies:
    def __init__(self, send, recv):
        self.send, self.recv, self.count = send, recv, 0

    def remote(self, src, dst, target):
        at = self.count
        self.count += 1
        copy = pltpu.make_async_remote_copy(
            src_ref=src,
            dst_ref=dst,
            send_sem=self.send.at[at],
            recv_sem=self.recv.at[at],
            device_id=target,
            device_id_type=MESH,
        )
        copy.start()
        return copy

    def local(self, src, dst):
        at = self.count
        self.count += 1
        copy = pltpu.make_async_copy(src, dst, self.send.at[at])
        copy.start()
        return copy


SEMS = 160


def kernel(
    orbitals, veff, trials, owners, levels, shift_index, out,
    phi, vfull, geff, masked, scattered, coef, band, fields, work_a, work_b, resp,
    r0a, r1a, r2a, r0b, r1b, r2b, r0c, r1c, r2c, s0a, s1a, s2a, s0b, s1b, s2b, final, slabs, z_a, z_b,
    send, recv,
):
    x, yh, yl, z, c = place()
    y = 2 * yh + yl
    orb, dom = lax.axis_index("orb"), lax.axis_index("dom")
    own = yl * 4 + z
    copies = Copies(send, recv)

    def along(dim, r):
        if dim == XP:
            return device((x + r) % 4, y, z, c)
        if dim == YP:
            return device(x, (y + r) % 4, z, c)
        return device(x, y, (z + r) % 4, c)

    sibling = device(x, y, z, 1 - c)

    barrier = pltpu.get_barrier_semaphore()
    peers = [((orb + r) % 16, dom) for r in range(1, 16)]
    peers += [(orb, (dom + r) % 8) for r in range(1, 8)]
    peers += [along(YP, 1), along(YP, 3)]
    for peer in peers:
        pl.semaphore_signal(barrier, inc=1, device_id=peer, device_id_type=MESH)
    pl.semaphore_wait(barrier, len(peers))

    chosen = [jnp.where(owners[app] == orb, 1.0, 0.0) for app in range(APPS)]
    for app in range(APPS):
        for i in range(8):
            masked[app, i] = trials[0, i] * chosen[app]
    spread = []
    for r in range(1, 16):
        to = (orb + r) % 16
        spread.append(copies.remote(masked.at[to % 2, to // 2], scattered.at[orb], (to, dom)))
    half = pl.ds(c * 32, 32)
    turn = 1 + 2 * yl
    order_y = (turn, 4 - turn, 2)

    def along_y(r):
        return device(x, (y + r) % 4, z, c)

    piece = veff.at[own, half]
    veff_y = [copies.remote(piece, geff.at[yh, x, yl, z, half], along_y(r)) for r in order_y]
    veff_own = copies.local(piece, geff.at[yh, x, yl, z, half])

    def move(flip, r):
        to = ((yh + flip) % 2) * 4 + (x + r) % 4
        source = ((yh + flip) % 2) * 4 + (x + 4 - r) % 4
        return source, copies.remote(orbitals.at[to], phi.at[c, dom], (orb, to))

    moved_near = [move(0, r) for r in (2, 1, 3)]
    phi_own = copies.local(orbitals.at[dom], phi.at[c, dom])
    phi_pair = [copies.remote(orbitals.at[dom], phi.at[c, dom], sibling)]
    gap = jnp.zeros((8, 128), jnp.float32) + levels[shift_index[dom]]
    for j, term in enumerate(coefficients(gap, 8 * 16)):
        coef[c, 8 * j : 8 * j + 8] = term
    coef_pair = copies.remote(coef.at[c], coef.at[c], sibling)
    distance = jnp.abs(
        lax.broadcasted_iota(jnp.int32, (256, 128), 0) % 128 - lax.broadcasted_iota(jnp.int32, (256, 128), 1)
    )
    band[...] = jnp.where(
        distance == 1, taps[0], jnp.where(distance == 2, taps[1], jnp.where(distance == 3, taps[2], 0.0))
    ).astype(jnp.bfloat16)

    zero_rows = jnp.zeros((8, 128), jnp.float32)
    zero_plane = jnp.zeros((80, 128), jnp.float32)
    for buffer in (fields, work_a, work_b):
        for k in range(2):
            for p in (0, 1, 2, 67, 68, 69):
                buffer[k, p] = zero_plane

            def border(p, carry, buffer=buffer, k=k):
                buffer[k, p, 0:8] = zero_rows
                buffer[k, p, 72:80] = zero_rows
                return carry

            lax.fori_loop(3, 67, border, 0)

    def wait(group):
        for copy in group:
            copy.wait()

    def ring(ref, h, rows):
        block = ref.at[h, :, :, z] if rows is None else ref.at[h, :, :, z, rows]
        return [copies.remote(block, block, along(ZP, r)) for r in (1, 3)]

    def relay(ref, h, rows, sends):
        wait(sends)
        started = []
        for l, zz, r in ((0, (z + 3) % 4, 1), (1, (z + 1) % 4, 3)):
            block = ref.at[h, :, l, zz] if rows is None else ref.at[h, :, l, zz, rows]
            started.append(copies.remote(block, block, along(ZP, r)))
        return started

    def forward(moves):
        for source, copy in moves:
            copy.wait()
            block = phi.at[c, source]
            phi_pair.append(copies.remote(block, block, sibling))

    other = 1 - yh

    def share(ref, h, rows):
        block = ref.at[h, x, :, z] if rows is None else ref.at[h, x, :, z, rows]
        return [copies.remote(block, block, along(XP, r)) for r in (2, 1, 3)]

    veff_own.wait()
    veff_y[0].wait()
    gx_own = share(geff, yh, half)
    wait(veff_y[1:])
    gx_oth = share(geff, other, half)
    scattered[orb] = masked[c, own]
    wait(spread)
    total = scattered[0]
    for g in range(1, 16):
        total = total + scattered[g]
    vfull[yh, x, yl, z] = total
    block = vfull.at[yh, x, yl, z]
    v_y = [copies.remote(block, block, along_y(r)) for r in order_y]
    wait(gx_own)
    g_own = ring(geff, yh, half)
    v_y[0].wait()
    vx_own = share(vfull, yh, None)
    wait(v_y[1:])
    vx_oth = share(vfull, other, None)
    moved_far = [move(1, 0)]
    wait(gx_oth)
    g_oth = ring(geff, other, half)
    wait(vx_own)
    v_own = ring(vfull, yh, None)
    wait(vx_oth)
    v_oth = ring(vfull, other, None)
    moved_far += [move(1, r) for r in (2, 1, 3)]
    g_own = relay(geff, yh, half, g_own)
    forward(moved_near)
    v_own = relay(vfull, yh, None, v_own)
    wait(g_own)
    block = geff.at[yh, :, :, :, half]
    g_pair = [copies.remote(block, block, sibling)]
    g_oth = relay(geff, other, half, g_oth)
    wait(v_own)
    phi_own.wait()
    wait(phi_pair)
    del phi_pair[:]
    coef_pair.wait()
    wait(g_pair)

    def start(p, norm):
        h, a, b, d = p // 32, (p // 8) % 4, (p // 4) % 2, p % 4
        v = vfull[h, a, b, d]
        for k in range(2):
            fields[k, p + 3, 8:72] = v * phi[k, p // 8, p % 8]
        geff[h, a, b, d] = (geff[h, a, b, d] + center_rest) * -180.0
        sq = v * v
        return norm + jnp.sum(sq.reshape(8, 8, 128), axis=0)

    def product(k, s, buf, src):
        block = src[k, pl.ds(s * 4 + 3, 4), 8:72].reshape(256, 128)
        high = block.astype(jnp.bfloat16)
        low = (block - high.astype(jnp.float32)).astype(jnp.bfloat16)
        buf[...] = jnp.dot(
            jnp.concatenate([high, low], axis=1), band[...], preferred_element_type=jnp.float32
        )

    def combine(k, s, buf, src, step, store):
        h, a, b = s // 8, (s // 2) % 4, s % 2
        weight = coef[k, step * 8 : step * 8 + 8]
        for r in range(0, 64, 8):
            column = [src[k, s * 4 + i, 8 + r : 16 + r] for i in range(10)]
            for i in range(4):
                value = column[i + 3]
                acc = buf[i * 64 + r : i * 64 + r + 8] + geff[h, a, b, i, r : r + 8] * value
                f = value if src is fields else fields[k, s * 4 + i + 3, 8 + r : 16 + r]
                acc = acc + weight * f
                for j in (1, 2, 3):
                    near = (column[i + 3 + j] + column[i + 3 - j]) + (
                        src[k, s * 4 + i + 3, 8 + r + j : 16 + r + j]
                        + src[k, s * 4 + i + 3, 8 + r - j : 16 + r - j]
                    )
                    acc = acc + (near if j == 3 else near * taps[j - 1])
                store(k, s, i, r, acc)

    def sweep(step, first, count):
        src, dst = ((fields, work_a), (work_a, work_b), (work_b, work_a), (work_a, None))[step]

        def keep(k, s, i, r, value):
            dst[k, s * 4 + i + 3, 8 + r : 16 + r] = value

        def respond(k, s, i, r, value):
            at = (s // 8, (s // 2) % 4, s % 2, i, slice(r, r + 8))
            value = value * (coef[k, 32:40] * phi[k, s // 2, (s % 2) * 4 + i, r : r + 8])
            resp[at] = value if k == 0 else resp[at] + value

        store = respond if dst is None else keep
        product(0, first, z_a, src)

        def chunk(n, carry):
            s = first + n
            product(1, s, z_b, src)
            combine(0, s, z_a, src, step, store)
            product(0, first + jnp.minimum(n + 1, count - 1), z_a, src)
            combine(1, s, z_b, src, step, store)
            return carry

        lax.fori_loop(0, count, chunk, 0)

    norm = jnp.zeros((8, 128), jnp.float32)

    def advance(step, done, until):
        sweep(step, jnp.where(yh == 0, done, 16 - until), until - done)

    norm = lax.fori_loop(32 * yh, 32 * yh + 32, start, norm)
    advance(0, 0, 7)
    v_oth = relay(vfull, other, None, v_oth)
    advance(1, 0, 6)
    wait(g_oth)
    block = geff.at[other, :, :, :, half]
    g_pair = [copies.remote(block, block, sibling)]
    forward(moved_far[:2])
    advance(2, 0, 5)
    forward(moved_far[2:])
    advance(3, 0, 4)
    wait(v_oth)
    wait(g_pair)
    wait(phi_pair)
    norm = lax.fori_loop(32 * other, 32 * other + 32, start, norm)
    for step in range(4):
        advance(step, 7 - step, 11 - step)
    scale = lax.rsqrt(jnp.sum(norm, keepdims=True) * (1.0 / 524288) + norm_epsilon)
    def part(dim, r, ref, kept):
        if dim == XP:
            where = {"x": (x + r) % 4}
        elif dim == YP:
            to = (y + r) % 4
            where = {"yh": to // 2, "yl": to % 2}
        else:
            where = {"z": (z + r) % 4}
        return ref.at[tuple(where.get(name, slice(None)) for name in kept)]

    names = {XP: ("x",), YP: ("yh", "yl"), ZP: ("z",)}
    orders = ((ZP, YP, XP), (YP, XP, ZP), (XP, ZP, YP))
    stages = ((r0a, r1a, r2a), (r0b, r1b, r2b), (r0c, r1c, r2c))
    sums = ((s0a, s1a, s2a), (s0b, s1b, s2b))
    kept = [("yh", "x", "yl", "z") for _ in GROUPS]
    current = [resp.at[:, :, :, :, first : first + count] for first, count in GROUPS]
    started = [[], [], []]

    def leave(h, turns):
        rows = [pl.ds(first, count) for first, count in GROUPS]
        for r in (2, 1, 3):
            started[0].append(
                copies.remote(resp.at[h, :, :, (z + r) % 4, rows[0]], r0a.at[r - 1, h], along(ZP, r))
            )
            started[2].append(
                copies.remote(resp.at[h, (x + r) % 4, :, :, rows[2]], r2a.at[r - 1, h], along(XP, r))
            )
        for r in turns:
            started[1].append(copies.remote(part(YP, r, current[1], kept[1]), r1a.at[r - 1], along_y(r)))

    leave(yh, (turn,))
    for step in range(4):
        advance(step, 11 - step, 16)
    leave(other, (4 - turn, 2))
    scale = lax.rsqrt(jnp.sum(norm, keepdims=True) * (1.0 / 524288) + norm_epsilon)
    for stage in range(3):
        if stage > 0:
            started = []
            for q in range(3):
                dim = orders[q][stage]
                started.append(
                    [
                        copies.remote(part(dim, r, current[q], kept[q]), stages[stage][q].at[r - 1], along(dim, r))
                        for r in (2, 1, 3)
                    ]
                )
        for q in range(3):
            dim = orders[q][stage]
            wait(started[q])
            received = stages[stage][q]
            mine = part(dim, 0, current[q], kept[q])
            kept[q] = tuple(name for name in kept[q] if name not in names[dim])
            first, count = GROUPS[q]
            if stage == 2:
                final[first : first + count] = ((mine[...] + received[0]) + (received[1] + received[2])) * scale
            else:
                sums[stage][q][...] = (mine[...] + received[0]) + (received[1] + received[2])
                current[q] = sums[stage][q]

    slabs[c, own] = final[...]
    shared, passed = [], [copies.remote(final, slabs.at[c, own], sibling)]
    for r in range(1, 8):
        to = (own + r) % 8
        shared.append(copies.remote(final, slabs.at[c, own], (to * 2 + c, dom)))
    for r in range(1, 8):
        shared[r - 1].wait()
        block = slabs.at[c, (own - r + 8) % 8]
        passed.append(copies.remote(block, block, sibling))
    wait(passed)
    for i in range(8):
        out[0, i] = slabs[0, i] * chosen[0] + slabs[1, i] * chosen[1]


def coefficients(level_gap, orbital_count):
    ratio_q = (center_depth + level_gap) * inverse_half
    root_term = jnp.sqrt(ratio_q * ratio_q - 1.0)
    decay = ratio_q - root_term
    c0 = -inverse_half / root_term
    c1 = c0 * (-2.0 * decay)
    c2 = c1 * -decay
    c3 = c2 * -decay
    c4 = c3 * -decay
    d0, d1, d2, d3, d4 = c0 - c2 + c4, c1 - 3.0 * c3, 2.0 * c2 - 8.0 * c4, 4.0 * c3, 8.0 * c4
    inverse = 1.0 / d4
    return [
        d3 * inverse * (1.0 / beta),
        d2 * inverse * (1.0 / beta**2),
        d1 * inverse * (1.0 / beta**3),
        d0 * inverse * (1.0 / beta**4),
        d4 * (beta**4 * 4.0 / orbital_count),
    ]


def per_device(orbitals, veff, trials, owners, levels, shift_index):
    f32 = jnp.float32
    vm = lambda *shape: pltpu.VMEM(shape, f32)
    full = (2, 4, 2, 4, 64, 128)
    return pl.pallas_call(
        kernel,
        out_shape=jax.ShapeDtypeStruct((1, 8, 64, 128), f32),
        in_specs=[
            pl.BlockSpec(memory_space=pl.ANY),
            pl.BlockSpec(memory_space=pl.ANY),
            pl.BlockSpec(memory_space=pltpu.VMEM),
            pl.BlockSpec(memory_space=pltpu.SMEM),
            pl.BlockSpec(memory_space=pltpu.SMEM),
            pl.BlockSpec(memory_space=pltpu.SMEM),
        ],
        out_specs=pl.BlockSpec(memory_space=pltpu.VMEM),
        scratch_shapes=[
            vm(2, 8, 8, 64, 128),
            vm(*full),
            vm(*full),
            vm(2, 8, 64, 128),
            vm(16, 64, 128),
            vm(2, 40, 128),
            pltpu.VMEM((256, 128), jnp.bfloat16),
            vm(2, 70, 80, 128),
            vm(2, 70, 80, 128),
            vm(2, 70, 80, 128),
            vm(*full),
            vm(3, 2, 4, 2, 24, 128),
            vm(3, 4, 4, 24, 128),
            vm(3, 2, 2, 4, 16, 128),
            vm(3, 4, 24, 128),
            vm(3, 4, 24, 128),
            vm(3, 2, 2, 16, 128),
            vm(3, 24, 128),
            vm(3, 24, 128),
            vm(3, 16, 128),
            vm(2, 4, 2, 24, 128),
            vm(4, 4, 24, 128),
            vm(2, 2, 4, 16, 128),
            vm(4, 24, 128),
            vm(4, 24, 128),
            vm(2, 2, 16, 128),
            vm(64, 128),
            vm(2, 8, 64, 128),
            vm(256, 128),
            vm(256, 128),
            pltpu.SemaphoreType.DMA((SEMS,)),
            pltpu.SemaphoreType.DMA((SEMS,)),
        ],
        compiler_params=pltpu.CompilerParams(
            collective_id=1, has_side_effects=True, vmem_limit_bytes=56 << 20
        ),
        name="response",
    )(orbitals, veff, trials, owners, levels, shift_index)


def solution(mesh):
    placed = (
        P("orb", "dom", None, None),
        P("dom", None, None),
        P("orb", "dom", None, None),
        P(),
        P(),
        P("orb"),
    )
    return jax.shard_map(
        per_device,
        mesh=mesh,
        in_specs=placed,
        out_specs=P("orb", "dom", None, None),
        check_vma=False,
    )
```

```python
import functools

import jax
import jax.numpy as jnp
from jax import lax
from jax.experimental import pallas as pl
from jax.experimental.pallas import tpu as pltpu
from jax.sharding import PartitionSpec as P

APPS = 2
SWEEPS = 4
MESH = pl.DeviceIdType.MESH

taps = (135.0, -13.5, 1.0)
inverse_half = 1.0 / 5.05
center_depth = 5.05
norm_epsilon = 1e-06
beta = -0.5 * inverse_half / 90.0
center_rest = 49.0 / 12.0 - 4.05

XP, YP, ZP = 2, 1, 0
GROUPS = ((0, 24), (24, 24), (48, 16))


def place():
    orb, dom = lax.axis_index("orb"), lax.axis_index("dom")
    return dom % 4, dom // 4, orb // 8, (orb // 2) % 4, orb % 2


def device(x, y, z, c):
    return ((y % 2) * 8 + z * 2 + c, (y // 2) * 4 + x)


class Copies:
    def __init__(self, send, recv):
        self.send, self.recv, self.count = send, recv, 0

    def remote(self, src, dst, target):
        at = self.count
        self.count += 1
        copy = pltpu.make_async_remote_copy(
            src_ref=src,
            dst_ref=dst,
            send_sem=self.send.at[at],
            recv_sem=self.recv.at[at],
            device_id=target,
            device_id_type=MESH,
        )
        copy.start()
        return copy

    def local(self, src, dst):
        at = self.count
        self.count += 1
        copy = pltpu.make_async_copy(src, dst, self.send.at[at])
        copy.start()
        return copy


SEMS = 160


def kernel(
    orbitals, veff, trials, owners, levels, shift_index, out,
    phi, vfull, geff, masked, scattered, coef, band, fields, work_a, work_b, resp,
    r0a, r1a, r2a, r0b, r1b, r2b, r0c, r1c, r2c, s0a, s1a, s2a, s0b, s1b, s2b, final, slabs, z_a, z_b,
    send, recv,
):
    x, yh, yl, z, c = place()
    y = 2 * yh + yl
    orb, dom = lax.axis_index("orb"), lax.axis_index("dom")
    own = yl * 4 + z
    copies = Copies(send, recv)

    def along(dim, r):
        if dim == XP:
            return device((x + r) % 4, y, z, c)
        if dim == YP:
            return device(x, (y + r) % 4, z, c)
        return device(x, y, (z + r) % 4, c)

    sibling = device(x, y, z, 1 - c)

    barrier = pltpu.get_barrier_semaphore()
    peers = [((orb + r) % 16, dom) for r in range(1, 16)]
    peers += [(orb, (dom + r) % 8) for r in range(1, 8)]
    peers += [along(YP, 1), along(YP, 3)]
    for peer in peers:
        pl.semaphore_signal(barrier, inc=1, device_id=peer, device_id_type=MESH)
    chosen = [jnp.where(owners[app] == orb, 1.0, 0.0) for app in range(APPS)]
    for app in range(APPS):
        for i in range(8):
            masked[app, i] = trials[0, i] * chosen[app]
    pl.semaphore_wait(barrier, len(peers))
    spread = []
    for r in range(1, 16):
        to = (orb + r) % 16
        spread.append(copies.remote(masked.at[to % 2, to // 2], scattered.at[orb], (to, dom)))
    half = pl.ds(c * 32, 32)
    turn = 1 + 2 * yl
    order_y = (turn, 4 - turn, 2)

    def along_y(r):
        return device(x, (y + r) % 4, z, c)

    piece = veff.at[own, half]
    veff_y = [copies.remote(piece, geff.at[yh, x, yl, z, half], along_y(r)) for r in order_y]
    veff_own = copies.local(piece, geff.at[yh, x, yl, z, half])

    def move(flip, r):
        to = ((yh + flip) % 2) * 4 + (x + r) % 4
        source = ((yh + flip) % 2) * 4 + (x + 4 - r) % 4
        return source, copies.remote(orbitals.at[to], phi.at[c, dom], (orb, to))

    moved_near = [move(0, r) for r in (2, 1, 3)]
    phi_own = copies.local(orbitals.at[dom], phi.at[c, dom])
    phi_pair = [copies.remote(orbitals.at[dom], phi.at[c, dom], sibling)]
    gap = jnp.zeros((8, 128), jnp.float32) + levels[shift_index[dom]]
    for j, term in enumerate(coefficients(gap, 8 * 16)):
        coef[c, 8 * j : 8 * j + 8] = term
    coef_pair = copies.remote(coef.at[c], coef.at[c], sibling)
    distance = jnp.abs(
        lax.broadcasted_iota(jnp.int32, (256, 128), 0) % 128 - lax.broadcasted_iota(jnp.int32, (256, 128), 1)
    )
    band[...] = jnp.where(
        distance == 1, taps[0], jnp.where(distance == 2, taps[1], jnp.where(distance == 3, taps[2], 0.0))
    ).astype(jnp.bfloat16)

    zero_rows = jnp.zeros((8, 128), jnp.float32)
    zero_plane = jnp.zeros((80, 128), jnp.float32)
    for buffer in (fields, work_a, work_b):
        for k in range(2):
            for p in (0, 1, 2, 67, 68, 69):
                buffer[k, p] = zero_plane

            def border(p, carry, buffer=buffer, k=k):
                buffer[k, p, 0:8] = zero_rows
                buffer[k, p, 72:80] = zero_rows
                return carry

            lax.fori_loop(3, 67, border, 0)

    def wait(group):
        for copy in group:
            copy.wait()

    def ring(ref, h, rows):
        block = ref.at[h, :, :, z] if rows is None else ref.at[h, :, :, z, rows]
        return [copies.remote(block, block, along(ZP, r)) for r in (1, 3)]

    def relay(ref, h, rows, sends):
        wait(sends)
        started = []
        for l, zz, r in ((0, (z + 3) % 4, 1), (1, (z + 1) % 4, 3)):
            block = ref.at[h, :, l, zz] if rows is None else ref.at[h, :, l, zz, rows]
            started.append(copies.remote(block, block, along(ZP, r)))
        return started

    def forward(moves):
        for source, copy in moves:
            copy.wait()
            block = phi.at[c, source]
            phi_pair.append(copies.remote(block, block, sibling))

    other = 1 - yh

    def share(ref, h, rows):
        block = ref.at[h, x, :, z] if rows is None else ref.at[h, x, :, z, rows]
        return [copies.remote(block, block, along(XP, r)) for r in (2, 1, 3)]

    veff_own.wait()
    veff_y[0].wait()
    gx_own = share(geff, yh, half)
    wait(veff_y[1:])
    gx_oth = share(geff, other, half)
    scattered[orb] = masked[c, own]
    wait(spread)
    total = scattered[0]
    for g in range(1, 16):
        total = total + scattered[g]
    vfull[yh, x, yl, z] = total
    block = vfull.at[yh, x, yl, z]
    v_y = [copies.remote(block, block, along_y(r)) for r in order_y]
    wait(gx_own)
    g_own = ring(geff, yh, half)
    v_y[0].wait()
    vx_own = share(vfull, yh, None)
    wait(v_y[1:])
    vx_oth = share(vfull, other, None)
    moved_far = [move(1, 0)]
    wait(gx_oth)
    g_oth = ring(geff, other, half)
    wait(vx_own)
    v_own = ring(vfull, yh, None)
    wait(vx_oth)
    moved_far += [move(1, r) for r in (2, 1, 3)]
    g_own = relay(geff, yh, half, g_own)
    v_own = relay(vfull, yh, None, v_own)
    v_oth = ring(vfull, other, None)
    forward(moved_near)
    wait(g_own)
    block = geff.at[yh, :, :, :, half]
    g_pair = [copies.remote(block, block, sibling)]
    g_oth = relay(geff, other, half, g_oth)
    wait(v_own)
    phi_own.wait()
    wait(phi_pair)
    del phi_pair[:]
    coef_pair.wait()
    wait(g_pair)

    def start(p, norm):
        h, a, b, d = p // 32, (p // 8) % 4, (p // 4) % 2, p % 4
        v = vfull[h, a, b, d]
        for k in range(2):
            fields[k, p + 3, 8:72] = v * phi[k, p // 8, p % 8]
        geff[h, a, b, d] = (geff[h, a, b, d] + center_rest) * -180.0
        sq = v * v
        return norm + jnp.sum(sq.reshape(8, 8, 128), axis=0)

    def product(k, s, buf, src):
        block = src[k, pl.ds(s * 4 + 3, 4), 8:72].reshape(256, 128)
        high = block.astype(jnp.bfloat16)
        low = (block - high.astype(jnp.float32)).astype(jnp.bfloat16)
        buf[...] = jnp.dot(
            jnp.concatenate([high, low], axis=1), band[...], preferred_element_type=jnp.float32
        )

    def combine(k, s, buf, src, step, store):
        h, a, b = s // 8, (s // 2) % 4, s % 2
        weight = coef[k, step * 8 : step * 8 + 8]
        for r in range(0, 64, 8):
            column = [src[k, s * 4 + i, 8 + r : 16 + r] for i in range(10)]
            for i in range(4):
                value = column[i + 3]
                acc = buf[i * 64 + r : i * 64 + r + 8] + geff[h, a, b, i, r : r + 8] * value
                f = value if src is fields else fields[k, s * 4 + i + 3, 8 + r : 16 + r]
                acc = acc + weight * f
                for j in (1, 2, 3):
                    near = (column[i + 3 + j] + column[i + 3 - j]) + (
                        src[k, s * 4 + i + 3, 8 + r + j : 16 + r + j]
                        + src[k, s * 4 + i + 3, 8 + r - j : 16 + r - j]
                    )
                    acc = acc + (near if j == 3 else near * taps[j - 1])
                store(k, s, i, r, acc)

    def sweep(step, first, count):
        src, dst = ((fields, work_a), (work_a, work_b), (work_b, work_a), (work_a, None))[step]

        def keep(k, s, i, r, value):
            dst[k, s * 4 + i + 3, 8 + r : 16 + r] = value

        def respond(k, s, i, r, value):
            at = (s // 8, (s // 2) % 4, s % 2, i, slice(r, r + 8))
            value = value * (coef[k, 32:40] * phi[k, s // 2, (s % 2) * 4 + i, r : r + 8])
            resp[at] = value if k == 0 else resp[at] + value

        store = respond if dst is None else keep
        product(0, first, z_a, src)

        def chunk(n, carry):
            s = first + n
            product(1, s, z_b, src)
            combine(0, s, z_a, src, step, store)
            product(0, first + jnp.minimum(n + 1, count - 1), z_a, src)
            combine(1, s, z_b, src, step, store)
            return carry

        lax.fori_loop(0, count, chunk, 0)

    norm = jnp.zeros((8, 128), jnp.float32)

    def advance(step, done, until):
        sweep(step, jnp.where(yh == 0, done, 16 - until), until - done)

    norm = lax.fori_loop(32 * yh, 32 * yh + 32, start, norm)
    advance(0, 0, 7)
    v_oth = relay(vfull, other, None, v_oth)
    advance(1, 0, 6)
    wait(g_oth)
    block = geff.at[other, :, :, :, half]
    g_pair = [copies.remote(block, block, sibling)]
    forward(moved_far[:2])
    advance(2, 0, 5)
    forward(moved_far[2:])
    advance(3, 0, 4)
    wait(v_oth)
    wait(g_pair)
    wait(phi_pair)
    norm = lax.fori_loop(32 * other, 32 * other + 32, start, norm)
    for step in range(4):
        advance(step, 7 - step, 11 - step)
    scale = lax.rsqrt(jnp.sum(norm, keepdims=True) * (1.0 / 524288) + norm_epsilon)
    def part(dim, r, ref, kept):
        if dim == XP:
            where = {"x": (x + r) % 4}
        elif dim == YP:
            to = (y + r) % 4
            where = {"yh": to // 2, "yl": to % 2}
        else:
            where = {"z": (z + r) % 4}
        return ref.at[tuple(where.get(name, slice(None)) for name in kept)]

    names = {XP: ("x",), YP: ("yh", "yl"), ZP: ("z",)}
    orders = ((ZP, YP, XP), (YP, XP, ZP), (XP, ZP, YP))
    stages = ((r0a, r1a, r2a), (r0b, r1b, r2b), (r0c, r1c, r2c))
    sums = ((s0a, s1a, s2a), (s0b, s1b, s2b))
    kept = [("yh", "x", "yl", "z") for _ in GROUPS]
    current = [resp.at[:, :, :, :, first : first + count] for first, count in GROUPS]
    started = [[], [], []]

    def leave(h, xs, count, turns):
        xs = pl.ds(xs, count)
        rows = [pl.ds(first, count) for first, count in GROUPS]
        for r in (2, 1, 3):
            started[0].append(
                copies.remote(resp.at[h, xs, :, (z + r) % 4, rows[0]], r0a.at[r - 1, h, xs], along(ZP, r))
            )
        for r in turns:
            to = (y + r) % 4
            started[1].append(
                copies.remote(resp.at[to // 2, xs, to % 2, :, rows[1]], r1a.at[r - 1, xs], along_y(r))
            )

    def leave_x(h):
        for r in (2, 1, 3):
            rows = pl.ds(GROUPS[2][0], GROUPS[2][1])
            started[2].append(
                copies.remote(resp.at[h, (x + r) % 4, :, :, rows], r2a.at[r - 1, h], along(XP, r))
            )

    leave(yh, 0, 4, (turn,))
    leave_x(yh)
    for step in range(4):
        advance(step, 11 - step, 15 - step)
    leave(other, 2 * yh, 2, (2, 4 - turn))
    for step in range(4):
        advance(step, 15 - step, 16)
    leave(other, 2 - 2 * yh, 2, (2, 4 - turn))
    leave_x(other)
    scale = lax.rsqrt(jnp.sum(norm, keepdims=True) * (1.0 / 524288) + norm_epsilon)
    for stage in range(3):
        if stage > 0:
            started = []
            for q in range(3):
                dim = orders[q][stage]
                started.append(
                    [
                        copies.remote(part(dim, r, current[q], kept[q]), stages[stage][q].at[r - 1], along(dim, r))
                        for r in (2, 1, 3)
                    ]
                )
        for q in range(3):
            dim = orders[q][stage]
            wait(started[q])
            received = stages[stage][q]
            mine = part(dim, 0, current[q], kept[q])
            kept[q] = tuple(name for name in kept[q] if name not in names[dim])
            first, count = GROUPS[q]
            if stage == 2:
                final[first : first + count] = ((mine[...] + received[0]) + (received[1] + received[2])) * scale
            else:
                sums[stage][q][...] = (mine[...] + received[0]) + (received[1] + received[2])
                current[q] = sums[stage][q]

    slabs[c, own] = final[...]
    shared, passed = [], [copies.remote(final, slabs.at[c, own], sibling)]
    for r in range(1, 8):
        to = (own + r) % 8
        shared.append(copies.remote(final, slabs.at[c, own], (to * 2 + c, dom)))
    for r in range(1, 8):
        shared[r - 1].wait()
        block = slabs.at[c, (own - r + 8) % 8]
        passed.append(copies.remote(block, block, sibling))
    wait(passed)
    for i in range(8):
        out[0, i] = slabs[0, i] * chosen[0] + slabs[1, i] * chosen[1]


def coefficients(level_gap, orbital_count):
    ratio_q = (center_depth + level_gap) * inverse_half
    root_term = jnp.sqrt(ratio_q * ratio_q - 1.0)
    decay = ratio_q - root_term
    c0 = -inverse_half / root_term
    c1 = c0 * (-2.0 * decay)
    c2 = c1 * -decay
    c3 = c2 * -decay
    c4 = c3 * -decay
    d0, d1, d2, d3, d4 = c0 - c2 + c4, c1 - 3.0 * c3, 2.0 * c2 - 8.0 * c4, 4.0 * c3, 8.0 * c4
    inverse = 1.0 / d4
    return [
        d3 * inverse * (1.0 / beta),
        d2 * inverse * (1.0 / beta**2),
        d1 * inverse * (1.0 / beta**3),
        d0 * inverse * (1.0 / beta**4),
        d4 * (beta**4 * 4.0 / orbital_count),
    ]


def per_device(orbitals, veff, trials, owners, levels, shift_index):
    f32 = jnp.float32
    vm = lambda *shape: pltpu.VMEM(shape, f32)
    full = (2, 4, 2, 4, 64, 128)
    return pl.pallas_call(
        kernel,
        out_shape=jax.ShapeDtypeStruct((1, 8, 64, 128), f32),
        in_specs=[
            pl.BlockSpec(memory_space=pl.ANY),
            pl.BlockSpec(memory_space=pl.ANY),
            pl.BlockSpec(memory_space=pltpu.VMEM),
            pl.BlockSpec(memory_space=pltpu.SMEM),
            pl.BlockSpec(memory_space=pltpu.SMEM),
            pl.BlockSpec(memory_space=pltpu.SMEM),
        ],
        out_specs=pl.BlockSpec(memory_space=pltpu.VMEM),
        scratch_shapes=[
            vm(2, 8, 8, 64, 128),
            vm(*full),
            vm(*full),
            vm(2, 8, 64, 128),
            vm(16, 64, 128),
            vm(2, 40, 128),
            pltpu.VMEM((256, 128), jnp.bfloat16),
            vm(2, 70, 80, 128),
            vm(2, 70, 80, 128),
            vm(2, 70, 80, 128),
            vm(*full),
            vm(3, 2, 4, 2, 24, 128),
            vm(3, 4, 4, 24, 128),
            vm(3, 2, 2, 4, 16, 128),
            vm(3, 4, 24, 128),
            vm(3, 4, 24, 128),
            vm(3, 2, 2, 16, 128),
            vm(3, 24, 128),
            vm(3, 24, 128),
            vm(3, 16, 128),
            vm(2, 4, 2, 24, 128),
            vm(4, 4, 24, 128),
            vm(2, 2, 4, 16, 128),
            vm(4, 24, 128),
            vm(4, 24, 128),
            vm(2, 2, 16, 128),
            vm(64, 128),
            vm(2, 8, 64, 128),
            vm(256, 128),
            vm(256, 128),
            pltpu.SemaphoreType.DMA((SEMS,)),
            pltpu.SemaphoreType.DMA((SEMS,)),
        ],
        compiler_params=pltpu.CompilerParams(
            collective_id=1, has_side_effects=True, vmem_limit_bytes=56 << 20
        ),
        name="response",
    )(orbitals, veff, trials, owners, levels, shift_index)


def solution(mesh):
    placed = (
        P("orb", "dom", None, None),
        P("dom", None, None),
        P("orb", "dom", None, None),
        P(),
        P(),
        P("orb"),
    )
    return jax.shard_map(
        per_device,
        mesh=mesh,
        in_specs=placed,
        out_specs=P("orb", "dom", None, None),
        check_vma=False,
    )
```

```python
import functools

import jax
import jax.numpy as jnp
from jax import lax
from jax.experimental import pallas as pl
from jax.experimental.pallas import tpu as pltpu
from jax.sharding import PartitionSpec as P

APPS = 2
SWEEPS = 4
MESH = pl.DeviceIdType.MESH

taps = (135.0, -13.5, 1.0)
inverse_half = 1.0 / 5.05
center_depth = 5.05
norm_epsilon = 1e-06
beta = -0.5 * inverse_half / 90.0
center_rest = 49.0 / 12.0 - 4.05

XP, YP, ZP = 2, 1, 0
GROUPS = ((0, 24), (24, 24), (48, 16))


def place():
    orb, dom = lax.axis_index("orb"), lax.axis_index("dom")
    return dom % 4, dom // 4, orb // 8, (orb // 2) % 4, orb % 2


def device(x, y, z, c):
    return ((y % 2) * 8 + z * 2 + c, (y // 2) * 4 + x)


class Copies:
    def __init__(self, send, recv):
        self.send, self.recv, self.count = send, recv, 0

    def remote(self, src, dst, target):
        at = self.count
        self.count += 1
        copy = pltpu.make_async_remote_copy(
            src_ref=src,
            dst_ref=dst,
            send_sem=self.send.at[at],
            recv_sem=self.recv.at[at],
            device_id=target,
            device_id_type=MESH,
        )
        copy.start()
        return copy

    def local(self, src, dst):
        at = self.count
        self.count += 1
        copy = pltpu.make_async_copy(src, dst, self.send.at[at])
        copy.start()
        return copy


SEMS = 160


def kernel(
    orbitals, veff, trials, owners, levels, shift_index, out,
    phi, vfull, geff, masked, scattered, coef, band, fields, work_a, work_b, resp,
    r0a, r1a, r2a, r0b, r1b, r2b, r0c, r1c, r2c, s0a, s1a, s2a, s0b, s1b, s2b, final, slabs, *rest,
):
    send, recv = rest[-2:]
    shifted = (rest[0:2], rest[2:4], rest[4:6], rest[6:8])
    z_a, z_b = shifted[0]
    x, yh, yl, z, c = place()
    y = 2 * yh + yl
    orb, dom = lax.axis_index("orb"), lax.axis_index("dom")
    own = yl * 4 + z
    copies = Copies(send, recv)

    def along(dim, r):
        if dim == XP:
            return device((x + r) % 4, y, z, c)
        if dim == YP:
            return device(x, (y + r) % 4, z, c)
        return device(x, y, (z + r) % 4, c)

    sibling = device(x, y, z, 1 - c)

    barrier = pltpu.get_barrier_semaphore()
    peers = [((orb + r) % 16, dom) for r in range(1, 16)]
    peers += [(orb, (dom + r) % 8) for r in range(1, 8)]
    peers += [along(YP, 1), along(YP, 3)]
    for peer in peers:
        pl.semaphore_signal(barrier, inc=1, device_id=peer, device_id_type=MESH)
    chosen = [jnp.where(owners[app] == orb, 1.0, 0.0) for app in range(APPS)]
    for app in range(APPS):
        for i in range(8):
            masked[app, i] = trials[0, i] * chosen[app]
    pl.semaphore_wait(barrier, len(peers))
    spread = []
    for r in range(1, 16):
        to = (orb + r) % 16
        spread.append(copies.remote(masked.at[to % 2, to // 2], scattered.at[orb], (to, dom)))
    half = pl.ds(c * 32, 32)
    turn = 1 + 2 * yl
    order_y = (turn, 4 - turn, 2)

    def along_y(r):
        return device(x, (y + r) % 4, z, c)

    piece = veff.at[own, half]
    veff_y = [copies.remote(piece, geff.at[yh, x, yl, z, half], along_y(r)) for r in order_y]
    veff_own = copies.local(piece, geff.at[yh, x, yl, z, half])

    def move(flip, r):
        to = ((yh + flip) % 2) * 4 + (x + r) % 4
        source = ((yh + flip) % 2) * 4 + (x + 4 - r) % 4
        return source, copies.remote(orbitals.at[to], phi.at[c, dom], (orb, to))

    moved_near = [move(0, r) for r in (2, 1, 3)]
    phi_own = copies.local(orbitals.at[dom], phi.at[c, dom])
    phi_pair = [copies.remote(orbitals.at[dom], phi.at[c, dom], sibling)]
    gap = jnp.zeros((8, 128), jnp.float32) + levels[shift_index[dom]]
    for j, term in enumerate(coefficients(gap, 8 * 16)):
        coef[c, 8 * j : 8 * j + 8] = term
    coef_pair = copies.remote(coef.at[c], coef.at[c], sibling)
    distance = jnp.abs(
        lax.broadcasted_iota(jnp.int32, (256, 128), 0) % 128 - lax.broadcasted_iota(jnp.int32, (256, 128), 1)
    )
    band[...] = jnp.where(
        distance == 1, taps[0], jnp.where(distance == 2, taps[1], jnp.where(distance == 3, taps[2], 0.0))
    ).astype(jnp.bfloat16)

    zero_rows = jnp.zeros((8, 128), jnp.float32)
    zero_plane = jnp.zeros((80, 128), jnp.float32)
    for buffer in (fields, work_a, work_b):
        for k in range(2):
            for p in (0, 1, 2, 67, 68, 69):
                buffer[k, p] = zero_plane

            def border(p, carry, buffer=buffer, k=k):
                buffer[k, p, 0:8] = zero_rows
                buffer[k, p, 72:80] = zero_rows
                return carry

            lax.fori_loop(3, 67, border, 0)

    def wait(group):
        for copy in group:
            copy.wait()

    def ring(ref, h, rows):
        block = ref.at[h, :, :, z] if rows is None else ref.at[h, :, :, z, rows]
        return [copies.remote(block, block, along(ZP, r)) for r in (1, 3)]

    def relay(ref, h, rows, sends):
        wait(sends)
        started = []
        for l, zz, r in ((0, (z + 3) % 4, 1), (1, (z + 1) % 4, 3)):
            block = ref.at[h, :, l, zz] if rows is None else ref.at[h, :, l, zz, rows]
            started.append(copies.remote(block, block, along(ZP, r)))
        return started

    def forward(moves):
        for source, copy in moves:
            copy.wait()
            block = phi.at[c, source]
            phi_pair.append(copies.remote(block, block, sibling))

    other = 1 - yh

    def share(ref, h, rows):
        block = ref.at[h, x, :, z] if rows is None else ref.at[h, x, :, z, rows]
        return [copies.remote(block, block, along(XP, r)) for r in (2, 1, 3)]

    veff_own.wait()
    veff_y[0].wait()
    gx_own = share(geff, yh, half)
    wait(veff_y[1:])
    gx_oth = share(geff, other, half)
    scattered[orb] = masked[c, own]
    wait(spread)
    total = scattered[0]
    for g in range(1, 16):
        total = total + scattered[g]
    vfull[yh, x, yl, z] = total
    block = vfull.at[yh, x, yl, z]
    v_y = [copies.remote(block, block, along_y(r)) for r in order_y]
    wait(gx_own)
    g_own = ring(geff, yh, half)
    v_y[0].wait()
    vx_own = share(vfull, yh, None)
    wait(v_y[1:])
    vx_oth = share(vfull, other, None)
    moved_far = [move(1, 0)]
    wait(gx_oth)
    g_oth = ring(geff, other, half)
    wait(vx_own)
    v_own = ring(vfull, yh, None)
    wait(vx_oth)
    moved_far += [move(1, r) for r in (2, 1, 3)]
    g_own = relay(geff, yh, half, g_own)
    v_own = relay(vfull, yh, None, v_own)
    v_oth = ring(vfull, other, None)
    forward(moved_near)
    wait(g_own)
    block = geff.at[yh, :, :, :, half]
    g_pair = [copies.remote(block, block, sibling)]
    g_oth = relay(geff, other, half, g_oth)
    wait(v_own)
    phi_own.wait()
    wait(phi_pair)
    del phi_pair[:]
    coef_pair.wait()
    wait(g_pair)

    def start(p, norm):
        h, a, b, d = p // 32, (p // 8) % 4, (p // 4) % 2, p % 4
        v = vfull[h, a, b, d]
        for k in range(2):
            fields[k, p + 3, 8:72] = v * phi[k, p // 8, p % 8]
        geff[h, a, b, d] = (geff[h, a, b, d] + center_rest) * -180.0
        sq = v * v
        return norm + jnp.sum(sq.reshape(8, 8, 128), axis=0)

    def product(k, s, buf, src):
        block = src[k, pl.ds(s * 4 + 3, 4), 8:72].reshape(256, 128)
        high = block.astype(jnp.bfloat16)
        low = (block - high.astype(jnp.float32)).astype(jnp.bfloat16)
        buf[...] = jnp.dot(
            jnp.concatenate([high, low], axis=1), band[...], preferred_element_type=jnp.float32
        )

    def combine(k, s, buf, src, step, store):
        h, a, b = s // 8, (s // 2) % 4, s % 2
        weight = coef[k, step * 8 : step * 8 + 8]
        for r in range(0, 64, 8):
            column = [src[k, s * 4 + i, 8 + r : 16 + r] for i in range(10)]
            for i in range(4):
                value = column[i + 3]
                acc = buf[i * 64 + r : i * 64 + r + 8] + geff[h, a, b, i, r : r + 8] * value
                f = value if src is fields else fields[k, s * 4 + i + 3, 8 + r : 16 + r]
                acc = acc + weight * f
                for j in (1, 2, 3):
                    near = (column[i + 3 + j] + column[i + 3 - j]) + (
                        src[k, s * 4 + i + 3, 8 + r + j : 16 + r + j]
                        + src[k, s * 4 + i + 3, 8 + r - j : 16 + r - j]
                    )
                    acc = acc + (near if j == 3 else near * taps[j - 1])
                store(k, s, i, r, acc)

    flow = ((fields, work_a), (work_a, work_b), (work_b, work_a), (work_a, None))

    def storing(step):
        dst = flow[step][1]

        def keep(k, s, i, r, value):
            dst[k, s * 4 + i + 3, 8 + r : 16 + r] = value

        def respond(k, s, i, r, value):
            at = (s // 8, (s // 2) % 4, s % 2, i, slice(r, r + 8))
            value = value * (coef[k, 32:40] * phi[k, s // 2, (s % 2) * 4 + i, r : r + 8])
            resp[at] = value if k == 0 else resp[at] + value

        return respond if dst is None else keep

    def chunk_of(n):
        return jnp.where(yh == 0, n, 15 - n)

    def wave(m, carry):
        def dot(step, k, n):
            product(k, chunk_of(n), shifted[step][k], flow[step][0])

        def add(step, k):
            combine(k, chunk_of(m + 3 - step), shifted[step][k], flow[step][0], step, storing(step))

        for step, ahead, n in ((0, 2, m + 1), (1, 3, m), (2, 0, jnp.minimum(m + 4, 15)), (3, 1, jnp.minimum(m + 3, 15))):
            for k in range(2):
                dot(ahead, k, n)
                add(step, k)
        return carry

    def sweep(step, first, count):
        src, dst = flow[step]
        store = storing(step)
        product(0, first, z_a, src)

        def chunk(n, carry):
            s = first + n
            product(1, s, z_b, src)
            combine(0, s, z_a, src, step, store)
            product(0, first + jnp.minimum(n + 1, count - 1), z_a, src)
            combine(1, s, z_b, src, step, store)
            return carry

        lax.fori_loop(0, count, chunk, 0)

    norm = jnp.zeros((8, 128), jnp.float32)

    def advance(step, done, until):
        sweep(step, jnp.where(yh == 0, done, 16 - until), until - done)

    norm = lax.fori_loop(32 * yh, 32 * yh + 32, start, norm)
    advance(0, 0, 7)
    v_oth = relay(vfull, other, None, v_oth)
    advance(1, 0, 6)
    wait(g_oth)
    block = geff.at[other, :, :, :, half]
    g_pair = [copies.remote(block, block, sibling)]
    forward(moved_far[:2])
    advance(2, 0, 5)
    forward(moved_far[2:])
    advance(3, 0, 4)
    wait(v_oth)
    wait(g_pair)
    wait(phi_pair)
    norm = lax.fori_loop(32 * other, 32 * other + 32, start, norm)
    for step in range(2):
        for k in range(2):
            product(k, chunk_of(7 - step), shifted[step][k], flow[step][0])
    lax.fori_loop(4, 8, wave, 0)
    scale = lax.rsqrt(jnp.sum(norm, keepdims=True) * (1.0 / 524288) + norm_epsilon)
    def part(dim, r, ref, kept):
        if dim == XP:
            where = {"x": (x + r) % 4}
        elif dim == YP:
            to = (y + r) % 4
            where = {"yh": to // 2, "yl": to % 2}
        else:
            where = {"z": (z + r) % 4}
        return ref.at[tuple(where.get(name, slice(None)) for name in kept)]

    names = {XP: ("x",), YP: ("yh", "yl"), ZP: ("z",)}
    orders = ((ZP, YP, XP), (YP, XP, ZP), (XP, ZP, YP))
    stages = ((r0a, r1a, r2a), (r0b, r1b, r2b), (r0c, r1c, r2c))
    sums = ((s0a, s1a, s2a), (s0b, s1b, s2b))
    kept = [("yh", "x", "yl", "z") for _ in GROUPS]
    current = [resp.at[:, :, :, :, first : first + count] for first, count in GROUPS]
    started = [[], [], []]

    def leave(h, xs, count, turns):
        xs = pl.ds(xs, count)
        rows = [pl.ds(first, count) for first, count in GROUPS]
        for r in (2, 1, 3):
            started[0].append(
                copies.remote(resp.at[h, xs, :, (z + r) % 4, rows[0]], r0a.at[r - 1, h, xs], along(ZP, r))
            )
        for r in turns:
            to = (y + r) % 4
            started[1].append(
                copies.remote(resp.at[to // 2, xs, to % 2, :, rows[1]], r1a.at[r - 1, xs], along_y(r))
            )

    def leave_x(h):
        for r in (2, 1, 3):
            rows = pl.ds(GROUPS[2][0], GROUPS[2][1])
            started[2].append(
                copies.remote(resp.at[h, (x + r) % 4, :, :, rows], r2a.at[r - 1, h], along(XP, r))
            )

    leave(yh, 0, 4, (turn,))
    leave_x(yh)
    lax.fori_loop(8, 12, wave, 0)
    leave(other, 2 * yh, 2, (2, 4 - turn))
    lax.fori_loop(12, 13, wave, 0)
    for step in (1, 2, 3):
        advance(step, 16 - step, 16)
    leave(other, 2 - 2 * yh, 2, (2, 4 - turn))
    leave_x(other)
    scale = lax.rsqrt(jnp.sum(norm, keepdims=True) * (1.0 / 524288) + norm_epsilon)
    for stage in range(3):
        if stage > 0:
            started = []
            for q in range(3):
                dim = orders[q][stage]
                started.append(
                    [
                        copies.remote(part(dim, r, current[q], kept[q]), stages[stage][q].at[r - 1], along(dim, r))
                        for r in (2, 1, 3)
                    ]
                )
        for q in range(3):
            dim = orders[q][stage]
            wait(started[q])
            received = stages[stage][q]
            mine = part(dim, 0, current[q], kept[q])
            kept[q] = tuple(name for name in kept[q] if name not in names[dim])
            first, count = GROUPS[q]
            if stage == 2:
                final[first : first + count] = ((mine[...] + received[0]) + (received[1] + received[2])) * scale
            else:
                sums[stage][q][...] = (mine[...] + received[0]) + (received[1] + received[2])
                current[q] = sums[stage][q]

    slabs[c, own] = final[...]
    shared, passed = [], [copies.remote(final, slabs.at[c, own], sibling)]
    for r in range(1, 8):
        to = (own + r) % 8
        shared.append(copies.remote(final, slabs.at[c, own], (to * 2 + c, dom)))
    for r in range(1, 8):
        shared[r - 1].wait()
        block = slabs.at[c, (own - r + 8) % 8]
        passed.append(copies.remote(block, block, sibling))
    wait(passed)
    for i in range(8):
        out[0, i] = slabs[0, i] * chosen[0] + slabs[1, i] * chosen[1]


def coefficients(level_gap, orbital_count):
    ratio_q = (center_depth + level_gap) * inverse_half
    root_term = jnp.sqrt(ratio_q * ratio_q - 1.0)
    decay = ratio_q - root_term
    c0 = -inverse_half / root_term
    c1 = c0 * (-2.0 * decay)
    c2 = c1 * -decay
    c3 = c2 * -decay
    c4 = c3 * -decay
    d0, d1, d2, d3, d4 = c0 - c2 + c4, c1 - 3.0 * c3, 2.0 * c2 - 8.0 * c4, 4.0 * c3, 8.0 * c4
    inverse = 1.0 / d4
    return [
        d3 * inverse * (1.0 / beta),
        d2 * inverse * (1.0 / beta**2),
        d1 * inverse * (1.0 / beta**3),
        d0 * inverse * (1.0 / beta**4),
        d4 * (beta**4 * 4.0 / orbital_count),
    ]


def per_device(orbitals, veff, trials, owners, levels, shift_index):
    f32 = jnp.float32
    vm = lambda *shape: pltpu.VMEM(shape, f32)
    full = (2, 4, 2, 4, 64, 128)
    return pl.pallas_call(
        kernel,
        out_shape=jax.ShapeDtypeStruct((1, 8, 64, 128), f32),
        in_specs=[
            pl.BlockSpec(memory_space=pl.ANY),
            pl.BlockSpec(memory_space=pl.ANY),
            pl.BlockSpec(memory_space=pltpu.VMEM),
            pl.BlockSpec(memory_space=pltpu.SMEM),
            pl.BlockSpec(memory_space=pltpu.SMEM),
            pl.BlockSpec(memory_space=pltpu.SMEM),
        ],
        out_specs=pl.BlockSpec(memory_space=pltpu.VMEM),
        scratch_shapes=[
            vm(2, 8, 8, 64, 128),
            vm(*full),
            vm(*full),
            vm(2, 8, 64, 128),
            vm(16, 64, 128),
            vm(2, 40, 128),
            pltpu.VMEM((256, 128), jnp.bfloat16),
            vm(2, 70, 80, 128),
            vm(2, 70, 80, 128),
            vm(2, 70, 80, 128),
            vm(*full),
            vm(3, 2, 4, 2, 24, 128),
            vm(3, 4, 4, 24, 128),
            vm(3, 2, 2, 4, 16, 128),
            vm(3, 4, 24, 128),
            vm(3, 4, 24, 128),
            vm(3, 2, 2, 16, 128),
            vm(3, 24, 128),
            vm(3, 24, 128),
            vm(3, 16, 128),
            vm(2, 4, 2, 24, 128),
            vm(4, 4, 24, 128),
            vm(2, 2, 4, 16, 128),
            vm(4, 24, 128),
            vm(4, 24, 128),
            vm(2, 2, 16, 128),
            vm(64, 128),
            vm(2, 8, 64, 128),
            *[vm(256, 128) for _ in range(8)],
            pltpu.SemaphoreType.DMA((SEMS,)),
            pltpu.SemaphoreType.DMA((SEMS,)),
        ],
        compiler_params=pltpu.CompilerParams(
            collective_id=1, has_side_effects=True, vmem_limit_bytes=56 << 20
        ),
        name="response",
    )(orbitals, veff, trials, owners, levels, shift_index)


def solution(mesh):
    placed = (
        P("orb", "dom", None, None),
        P("dom", None, None),
        P("orb", "dom", None, None),
        P(),
        P(),
        P("orb"),
    )
    return jax.shard_map(
        per_device,
        mesh=mesh,
        in_specs=placed,
        out_specs=P("orb", "dom", None, None),
        check_vma=False,
    )
```

```python
import functools

import jax
import jax.numpy as jnp
from jax import lax
from jax.experimental import pallas as pl
from jax.experimental.pallas import tpu as pltpu
from jax.sharding import PartitionSpec as P

APPS = 2
SWEEPS = 4
MESH = pl.DeviceIdType.MESH

taps = (135.0, -13.5, 1.0)
inverse_half = 1.0 / 5.05
center_depth = 5.05
norm_epsilon = 1e-06
beta = -0.5 * inverse_half / 90.0
center_rest = 49.0 / 12.0 - 4.05

XP, YP, ZP = 2, 1, 0
GROUPS = ((0, 24), (24, 24), (48, 16))


def place():
    orb, dom = lax.axis_index("orb"), lax.axis_index("dom")
    return dom % 4, dom // 4, orb // 8, (orb // 2) % 4, orb % 2


def device(x, y, z, c):
    return ((y % 2) * 8 + z * 2 + c, (y // 2) * 4 + x)


class Copies:
    def __init__(self, send, recv):
        self.send, self.recv, self.count = send, recv, 0

    def remote(self, src, dst, target):
        at = self.count
        self.count += 1
        copy = pltpu.make_async_remote_copy(
            src_ref=src,
            dst_ref=dst,
            send_sem=self.send.at[at],
            recv_sem=self.recv.at[at],
            device_id=target,
            device_id_type=MESH,
        )
        copy.start()
        return copy

    def local(self, src, dst):
        at = self.count
        self.count += 1
        copy = pltpu.make_async_copy(src, dst, self.send.at[at])
        copy.start()
        return copy


SEMS = 160


def kernel(
    orbitals, veff, trials, owners, levels, shift_index, out,
    phi, vfull, geff, masked, scattered, coef, band, fields, work_a, work_b, resp,
    r0a, r1a, r2a, r0b, r1b, r2b, r0c, r1c, r2c, s0a, s1a, s2a, s0b, s1b, s2b, final, slabs, *rest,
):
    send, recv = rest[-2:]
    shifted = (rest[0:2], rest[2:4], rest[4:6], rest[6:8])
    z_a, z_b = shifted[0]
    x, yh, yl, z, c = place()
    y = 2 * yh + yl
    orb, dom = lax.axis_index("orb"), lax.axis_index("dom")
    own = yl * 4 + z
    copies = Copies(send, recv)

    def along(dim, r):
        if dim == XP:
            return device((x + r) % 4, y, z, c)
        if dim == YP:
            return device(x, (y + r) % 4, z, c)
        return device(x, y, (z + r) % 4, c)

    sibling = device(x, y, z, 1 - c)

    barrier = pltpu.get_barrier_semaphore()
    peers = [((orb + r) % 16, dom) for r in range(1, 16)]
    peers += [(orb, (dom + r) % 8) for r in range(1, 8)]
    peers += [along(YP, 1), along(YP, 3)]
    for peer in peers:
        pl.semaphore_signal(barrier, inc=1, device_id=peer, device_id_type=MESH)
    chosen = [jnp.where(owners[app] == orb, 1.0, 0.0) for app in range(APPS)]
    for app in range(APPS):
        for i in range(8):
            masked[app, i] = trials[0, i] * chosen[app]
    pl.semaphore_wait(barrier, len(peers))
    spread = []
    for r in range(1, 16):
        to = (orb + r) % 16
        spread.append(copies.remote(masked.at[to % 2, to // 2], scattered.at[orb], (to, dom)))
    half = pl.ds(c * 32, 32)
    turn = 1 + 2 * yl
    order_y = (turn, 4 - turn, 2)

    def along_y(r):
        return device(x, (y + r) % 4, z, c)

    piece = veff.at[own, half]
    veff_y = [copies.remote(piece, geff.at[yh, x, yl, z, half], along_y(r)) for r in order_y]
    veff_own = copies.local(piece, geff.at[yh, x, yl, z, half])

    def move(flip, r):
        to = ((yh + flip) % 2) * 4 + (x + r) % 4
        source = ((yh + flip) % 2) * 4 + (x + 4 - r) % 4
        return source, copies.remote(orbitals.at[to], phi.at[c, dom], (orb, to))

    moved_near = [move(0, r) for r in (2, 1, 3)]
    phi_own = copies.local(orbitals.at[dom], phi.at[c, dom])
    phi_pair = [copies.remote(orbitals.at[dom], phi.at[c, dom], sibling)]
    gap = jnp.zeros((8, 128), jnp.float32) + levels[shift_index[dom]]
    for j, term in enumerate(coefficients(gap, 8 * 16)):
        coef[c, 8 * j : 8 * j + 8] = term
    coef_pair = copies.remote(coef.at[c], coef.at[c], sibling)
    distance = jnp.abs(
        lax.broadcasted_iota(jnp.int32, (256, 128), 0) % 128 - lax.broadcasted_iota(jnp.int32, (256, 128), 1)
    )
    band[...] = jnp.where(
        distance == 1, taps[0], jnp.where(distance == 2, taps[1], jnp.where(distance == 3, taps[2], 0.0))
    ).astype(jnp.bfloat16)

    zero_rows = jnp.zeros((8, 128), jnp.float32)
    zero_plane = jnp.zeros((80, 128), jnp.float32)
    for buffer in (fields, work_a, work_b):
        for k in range(2):
            for p in (0, 1, 2, 67, 68, 69):
                buffer[k, p] = zero_plane

            def border(p, carry, buffer=buffer, k=k):
                buffer[k, p, 0:8] = zero_rows
                buffer[k, p, 72:80] = zero_rows
                return carry

            lax.fori_loop(3, 67, border, 0)

    def wait(group):
        for copy in group:
            copy.wait()

    def ring(ref, h, rows):
        block = ref.at[h, :, :, z] if rows is None else ref.at[h, :, :, z, rows]
        return [copies.remote(block, block, along(ZP, r)) for r in (1, 3)]

    def relay(ref, h, rows, sends):
        wait(sends)
        started = []
        for l, zz, r in ((0, (z + 3) % 4, 1), (1, (z + 1) % 4, 3)):
            block = ref.at[h, :, l, zz] if rows is None else ref.at[h, :, l, zz, rows]
            started.append(copies.remote(block, block, along(ZP, r)))
        return started

    def forward(moves):
        for source, copy in moves:
            copy.wait()
            block = phi.at[c, source]
            phi_pair.append(copies.remote(block, block, sibling))

    other = 1 - yh

    def share(ref, h, rows):
        block = ref.at[h, x, :, z] if rows is None else ref.at[h, x, :, z, rows]
        return [copies.remote(block, block, along(XP, r)) for r in (2, 1, 3)]

    veff_own.wait()
    veff_y[0].wait()
    gx_own = share(geff, yh, half)
    wait(veff_y[1:])
    gx_oth = share(geff, other, half)
    scattered[orb] = masked[c, own]
    wait(spread)
    total = scattered[0]
    for g in range(1, 16):
        total = total + scattered[g]
    vfull[yh, x, yl, z] = total
    block = vfull.at[yh, x, yl, z]
    v_y = [copies.remote(block, block, along_y(r)) for r in order_y]
    wait(gx_own)
    g_own = ring(geff, yh, half)
    v_y[0].wait()
    vx_own = share(vfull, yh, None)
    wait(v_y[1:])
    vx_oth = share(vfull, other, None)
    moved_far = [move(1, 0)]
    wait(gx_oth)
    g_oth = ring(geff, other, half)
    wait(vx_own)
    v_own = ring(vfull, yh, None)
    wait(vx_oth)
    moved_far += [move(1, r) for r in (2, 1, 3)]
    g_own = relay(geff, yh, half, g_own)
    v_own = relay(vfull, yh, None, v_own)
    v_oth = ring(vfull, other, None)
    forward(moved_near)
    wait(g_own)
    block = geff.at[yh, :, :, :, half]
    g_pair = [copies.remote(block, block, sibling)]
    g_oth = relay(geff, other, half, g_oth)
    wait(v_own)
    phi_own.wait()
    wait(phi_pair)
    del phi_pair[:]
    coef_pair.wait()
    wait(g_pair)

    def start(p, norm):
        h, a, b, d = p // 32, (p // 8) % 4, (p // 4) % 2, p % 4
        v = vfull[h, a, b, d]
        for k in range(2):
            fields[k, p + 3, 8:72] = v * phi[k, p // 8, p % 8]
        geff[h, a, b, d] = (geff[h, a, b, d] + center_rest) * -180.0
        sq = v * v
        return norm + jnp.sum(sq.reshape(8, 8, 128), axis=0)

    def product(k, s, buf, src):
        block = src[k, pl.ds(s * 4 + 3, 4), 8:72].reshape(256, 128)
        high = block.astype(jnp.bfloat16)
        low = (block - high.astype(jnp.float32)).astype(jnp.bfloat16)
        buf[...] = jnp.dot(
            jnp.concatenate([high, low], axis=1), band[...], preferred_element_type=jnp.float32
        )

    def combine(k, s, buf, src, step, store):
        h, a, b = s // 8, (s // 2) % 4, s % 2
        weight = coef[k, step * 8 : step * 8 + 8]
        for r in range(0, 64, 8):
            column = [src[k, s * 4 + i, 8 + r : 16 + r] for i in range(10)]
            for i in range(4):
                value = column[i + 3]
                acc = buf[i * 64 + r : i * 64 + r + 8] + geff[h, a, b, i, r : r + 8] * value
                f = value if src is fields else fields[k, s * 4 + i + 3, 8 + r : 16 + r]
                acc = acc + weight * f
                for j in (1, 2, 3):
                    near = (column[i + 3 + j] + column[i + 3 - j]) + (
                        src[k, s * 4 + i + 3, 8 + r + j : 16 + r + j]
                        + src[k, s * 4 + i + 3, 8 + r - j : 16 + r - j]
                    )
                    acc = acc + (near if j == 3 else near * taps[j - 1])
                store(k, s, i, r, acc)

    flow = ((fields, work_a), (work_a, work_b), (work_b, work_a), (work_a, None))

    def storing(step):
        dst = flow[step][1]

        def keep(k, s, i, r, value):
            dst[k, s * 4 + i + 3, 8 + r : 16 + r] = value

        def respond(k, s, i, r, value):
            at = (s // 8, (s // 2) % 4, s % 2, i, slice(r, r + 8))
            value = value * (coef[k, 32:40] * phi[k, s // 2, (s % 2) * 4 + i, r : r + 8])
            resp[at] = value if k == 0 else resp[at] + value

        return respond if dst is None else keep

    def chunk_of(n):
        return jnp.where(yh == 0, n, 15 - n)

    def wave(m, carry):
        def dot(step, k, n):
            product(k, chunk_of(n), shifted[step][k], flow[step][0])

        def add(step, k):
            combine(k, chunk_of(m + 3 - step), shifted[step][k], flow[step][0], step, storing(step))

        for step, ahead, n in ((0, 2, m + 1), (1, 3, m), (2, 0, jnp.minimum(m + 4, 15)), (3, 1, jnp.minimum(m + 3, 15))):
            for k in range(2):
                dot(ahead, k, n)
                add(step, k)
        return carry

    def sweep(step, first, count):
        src, dst = flow[step]
        store = storing(step)
        product(0, first, z_a, src)

        def chunk(n, carry):
            s = first + n
            product(1, s, z_b, src)
            combine(0, s, z_a, src, step, store)
            product(0, first + jnp.minimum(n + 1, count - 1), z_a, src)
            combine(1, s, z_b, src, step, store)
            return carry

        lax.fori_loop(0, count, chunk, 0)

    norm = jnp.zeros((8, 128), jnp.float32)

    def advance(step, done, until):
        sweep(step, jnp.where(yh == 0, done, 16 - until), until - done)

    norm = lax.fori_loop(32 * yh, 32 * yh + 32, start, norm)
    advance(0, 0, 7)
    v_oth = relay(vfull, other, None, v_oth)
    forward(moved_far[:1])
    advance(1, 0, 6)
    wait(g_oth)
    block = geff.at[other, :, :, :, half]
    g_pair = [copies.remote(block, block, sibling)]
    forward(moved_far[1:])
    advance(2, 0, 5)
    advance(3, 0, 4)
    wait(v_oth)
    wait(g_pair)
    wait(phi_pair)
    norm = lax.fori_loop(32 * other, 32 * other + 32, start, norm)
    for step in range(2):
        for k in range(2):
            product(k, chunk_of(7 - step), shifted[step][k], flow[step][0])
    lax.fori_loop(4, 8, wave, 0)
    scale = lax.rsqrt(jnp.sum(norm, keepdims=True) * (1.0 / 524288) + norm_epsilon)
    def part(dim, r, ref, kept):
        if dim == XP:
            where = {"x": (x + r) % 4}
        elif dim == YP:
            to = (y + r) % 4
            where = {"yh": to // 2, "yl": to % 2}
        else:
            where = {"z": (z + r) % 4}
        return ref.at[tuple(where.get(name, slice(None)) for name in kept)]

    names = {XP: ("x",), YP: ("yh", "yl"), ZP: ("z",)}
    orders = ((ZP, YP, XP), (YP, XP, ZP), (XP, ZP, YP))
    stages = ((r0a, r1a, r2a), (r0b, r1b, r2b), (r0c, r1c, r2c))
    sums = ((s0a, s1a, s2a), (s0b, s1b, s2b))
    kept = [("yh", "x", "yl", "z") for _ in GROUPS]
    current = [resp.at[:, :, :, :, first : first + count] for first, count in GROUPS]
    started = [[], [], []]

    def leave(h, xs, count, turns):
        xs = pl.ds(xs, count)
        rows = [pl.ds(first, count) for first, count in GROUPS]
        for r in (2, 1, 3):
            started[0].append(
                copies.remote(resp.at[h, xs, :, (z + r) % 4, rows[0]], r0a.at[r - 1, h, xs], along(ZP, r))
            )
        for r in turns:
            to = (y + r) % 4
            started[1].append(
                copies.remote(resp.at[to // 2, xs, to % 2, :, rows[1]], r1a.at[r - 1, xs], along_y(r))
            )

    def leave_x(h):
        for r in (2, 1, 3):
            rows = pl.ds(GROUPS[2][0], GROUPS[2][1])
            started[2].append(
                copies.remote(resp.at[h, (x + r) % 4, :, :, rows], r2a.at[r - 1, h], along(XP, r))
            )

    leave(yh, 0, 4, (turn,))
    leave_x(yh)
    lax.fori_loop(8, 12, wave, 0)
    leave(other, 2 * yh, 2, (2, 4 - turn))
    lax.fori_loop(12, 13, wave, 0)
    for step in (1, 2, 3):
        advance(step, 16 - step, 16)
    leave(other, 2 - 2 * yh, 2, (2, 4 - turn))
    leave_x(other)
    scale = lax.rsqrt(jnp.sum(norm, keepdims=True) * (1.0 / 524288) + norm_epsilon)
    for stage in range(3):
        if stage > 0:
            started = []
            for q in range(3):
                dim = orders[q][stage]
                started.append(
                    [
                        copies.remote(part(dim, r, current[q], kept[q]), stages[stage][q].at[r - 1], along(dim, r))
                        for r in (2, 1, 3)
                    ]
                )
        for q in range(3):
            dim = orders[q][stage]
            wait(started[q])
            received = stages[stage][q]
            mine = part(dim, 0, current[q], kept[q])
            kept[q] = tuple(name for name in kept[q] if name not in names[dim])
            first, count = GROUPS[q]
            if stage == 2:
                final[first : first + count] = ((mine[...] + received[0]) + (received[1] + received[2])) * scale
            else:
                sums[stage][q][...] = (mine[...] + received[0]) + (received[1] + received[2])
                current[q] = sums[stage][q]

    slabs[c, own] = final[...]
    shared, passed = [], [copies.remote(final, slabs.at[c, own], sibling)]
    for r in range(1, 8):
        to = (own + r) % 8
        shared.append(copies.remote(final, slabs.at[c, own], (to * 2 + c, dom)))
    for r in range(1, 8):
        shared[r - 1].wait()
        block = slabs.at[c, (own - r + 8) % 8]
        passed.append(copies.remote(block, block, sibling))
    wait(passed)
    for i in range(8):
        out[0, i] = slabs[0, i] * chosen[0] + slabs[1, i] * chosen[1]


def coefficients(level_gap, orbital_count):
    ratio_q = (center_depth + level_gap) * inverse_half
    root_term = jnp.sqrt(ratio_q * ratio_q - 1.0)
    decay = ratio_q - root_term
    c0 = -inverse_half / root_term
    c1 = c0 * (-2.0 * decay)
    c2 = c1 * -decay
    c3 = c2 * -decay
    c4 = c3 * -decay
    d0, d1, d2, d3, d4 = c0 - c2 + c4, c1 - 3.0 * c3, 2.0 * c2 - 8.0 * c4, 4.0 * c3, 8.0 * c4
    inverse = 1.0 / d4
    return [
        d3 * inverse * (1.0 / beta),
        d2 * inverse * (1.0 / beta**2),
        d1 * inverse * (1.0 / beta**3),
        d0 * inverse * (1.0 / beta**4),
        d4 * (beta**4 * 4.0 / orbital_count),
    ]


def per_device(orbitals, veff, trials, owners, levels, shift_index):
    f32 = jnp.float32
    vm = lambda *shape: pltpu.VMEM(shape, f32)
    full = (2, 4, 2, 4, 64, 128)
    return pl.pallas_call(
        kernel,
        out_shape=jax.ShapeDtypeStruct((1, 8, 64, 128), f32),
        in_specs=[
            pl.BlockSpec(memory_space=pl.ANY),
            pl.BlockSpec(memory_space=pl.ANY),
            pl.BlockSpec(memory_space=pltpu.VMEM),
            pl.BlockSpec(memory_space=pltpu.SMEM),
            pl.BlockSpec(memory_space=pltpu.SMEM),
            pl.BlockSpec(memory_space=pltpu.SMEM),
        ],
        out_specs=pl.BlockSpec(memory_space=pltpu.VMEM),
        scratch_shapes=[
            vm(2, 8, 8, 64, 128),
            vm(*full),
            vm(*full),
            vm(2, 8, 64, 128),
            vm(16, 64, 128),
            vm(2, 40, 128),
            pltpu.VMEM((256, 128), jnp.bfloat16),
            vm(2, 70, 80, 128),
            vm(2, 70, 80, 128),
            vm(2, 70, 80, 128),
            vm(*full),
            vm(3, 2, 4, 2, 24, 128),
            vm(3, 4, 4, 24, 128),
            vm(3, 2, 2, 4, 16, 128),
            vm(3, 4, 24, 128),
            vm(3, 4, 24, 128),
            vm(3, 2, 2, 16, 128),
            vm(3, 24, 128),
            vm(3, 24, 128),
            vm(3, 16, 128),
            vm(2, 4, 2, 24, 128),
            vm(4, 4, 24, 128),
            vm(2, 2, 4, 16, 128),
            vm(4, 24, 128),
            vm(4, 24, 128),
            vm(2, 2, 16, 128),
            vm(64, 128),
            vm(2, 8, 64, 128),
            *[vm(256, 128) for _ in range(8)],
            pltpu.SemaphoreType.DMA((SEMS,)),
            pltpu.SemaphoreType.DMA((SEMS,)),
        ],
        compiler_params=pltpu.CompilerParams(
            collective_id=1, has_side_effects=True, vmem_limit_bytes=56 << 20
        ),
        name="response",
    )(orbitals, veff, trials, owners, levels, shift_index)


def solution(mesh):
    placed = (
        P("orb", "dom", None, None),
        P("dom", None, None),
        P("orb", "dom", None, None),
        P(),
        P(),
        P("orb"),
    )
    return jax.shard_map(
        per_device,
        mesh=mesh,
        in_specs=placed,
        out_specs=P("orb", "dom", None, None),
        check_vma=False,
    )
```
